512 devices in a mesh: seq: 64 (over y, z), head: 8 (over x, core).
Axes of the slice: x: 4, y: 4, z: 16, core: 2. Of those that a mesh axis runs over, the one named last changes fastest.
Arguments:
- queries: bfloat16 [65536, 2048], P(('seq', 'head')), may hold values from -135 to 135
- keys: bfloat16 [65536, 2048], P(('seq', 'head')), may hold values from -4.5 to 4.5
- values: bfloat16 [65536, 2048], P(('seq', 'head')), may hold values from -4.5 to 4.5
- doc_ids: int32 [65536], P(('seq', 'head')), may hold values from 0 to 127, never falling along the last dimension, each value on 1 to 1025 neighbouring positions
Outputs:
- attended: bfloat16 [65536, 2048], P(('seq', 'head'))
The draws below stay inside these ranges and needn't reach their ends.
Inputs may be any that keep to these rules, and one draw needn't show every extreme that they name: `doc_ids`: never falling; every id from 0 to 127 names 1 to 1025 tokens, and one names exactly 1025.
All inputs are finite; a program needn't handle non-finite values.
Results may differ from the reference program's by a relative error of at most 0.0045.
Values may be sent and summed in bfloat16 or wider, within the bound.
No kernel may reach another device: no remote copies, remote signals or barrier semaphores. Data moves between devices by JAX's collectives and lax.ppermute only.
A program may use at most 64 MiB of HBM per device.

```python
import math
import jax
import jax.numpy as jnp
import numpy as np
from jax import lax

HD = 128
BLK = 1024
SPAN = 1
FEAT = 2048
SEQ = 65536
DOC_MAX = 1025
DOCS = 128


def shared_keys(key):
    return jnp.clip(jax.random.normal(key, (SEQ, FEAT), jnp.float32), -4.5, 4.5)


def draw_keys(key, part):
    common = shared_keys(key)
    return common.astype(jnp.bfloat16)


def draw_queries(key, part):
    key = jax.random.fold_in(key, 23)
    normal_key = jax.random.fold_in(key, 0)
    drawn = jnp.clip(jax.random.normal(normal_key, (SEQ, FEAT), jnp.float32), -4.5, 4.5)
    return drawn.astype(jnp.bfloat16)


def shard_levels(own_key, dims, pieces, least, high):
    def one(position, parts):
        heights = jax.random.uniform(jax.random.fold_in(jax.random.fold_in(own_key, 6), position), (parts,), jnp.float32, least / len(pieces), high / len(pieces))
        return jnp.repeat(jnp.exp(heights), dims[position] // parts).reshape((-1,) + (1,) * (len(dims) - position - 1))

    level = one(*pieces[0])
    for cut in pieces[1:]:
        level = level * one(*cut)
    return level


def split_up(amount, total, bound, lean):
    loads = [(1 << 20) // math.isqrt(grade ** lean) + 1 for grade in range(2, amount + 1)]
    surplus, holding = total - bound - (amount - 1), [1] * (amount - 1)
    while surplus > 0:
        free = [i for i in range(amount - 1) if holding[i] < bound]
        whole, remaining = sum([loads[i] for i in free]), surplus
        for i in free:
            extra = min(bound - holding[i], max(1, remaining * loads[i] // whole), surplus)
            holding[i] = holding[i] + extra
            surplus = surplus - extra
    return np.array([bound] + holding)


def ragged(stream_key, amount, total, most, skew):
    if amount == 2:
        one = jax.random.randint(stream_key, (), max(1, total - most), min(most, total - 1) + 1)
        return jnp.stack([one, total - one])
    lengths = jnp.asarray(split_up(amount, total, most, skew), jnp.int32)
    pairs = (amount - 1) // 2
    donor, taker = lengths[1:1 + 2 * pairs:2], lengths[2:2 + 2 * pairs:2]
    margin = jnp.minimum(donor - 1, most - taker)
    passed = jax.random.randint(jax.random.fold_in(stream_key, 1), (pairs,), 0, 1 << 20) % (margin + 1)
    lengths = lengths.at[1:1 + 2 * pairs:2].set(donor - passed).at[2:2 + 2 * pairs:2].set(taker + passed)
    return lengths[jax.random.permutation(jax.random.fold_in(stream_key, 2), amount)]


def scatter_about(key, extent, deviation, limit, shards=(), kind=jnp.bfloat16):
    values = deviation * jax.random.normal(key, extent, jnp.float32)
    if shards:
        values = values * shard_levels(key, extent, shards, -0.22, 0.18)
    return jnp.clip(values, -limit, limit).astype(kind)


def setup_inputs(seed: int = 0) -> dict:
    key_list = jax.random.split(jax.random.key(seed), 5)
    queries = draw_queries(jax.random.fold_in(key_list[4], 71), 0)
    keys = draw_keys(jax.random.fold_in(key_list[4], 71), 0)
    values = scatter_about(key_list[2], (SEQ, FEAT), 1.0, 4.5, ((0, 512),))
    doc_ids = jnp.searchsorted(jnp.cumsum(ragged(key_list[3], DOCS, SEQ, DOC_MAX, 2)), jnp.arange(SEQ), side="right").astype(jnp.int32)
    return {"queries": queries, "keys": keys, "values": values, "doc_ids": doc_ids}


def score_tiles(query_rows, key_rows, value_rows, query_ids, key_ids):
    row_count = query_rows.shape[0]
    head_count = query_rows.shape[1] // HD
    same_doc = query_ids[:, None] == key_ids[None, :]
    score_scale = 1.0 / math.sqrt(HD)

    def live_tile():
        query_heads = query_rows.reshape(row_count, head_count, HD).astype(jnp.float32)
        key_heads = key_rows.reshape(row_count, head_count, HD).astype(jnp.float32)
        value_heads = value_rows.reshape(row_count, head_count, HD).astype(jnp.float32)
        scores = jnp.einsum('qhd,khd->hqk', query_heads, key_heads) * score_scale
        row_max = lax.optimization_barrier(jnp.max(jnp.where(same_doc[None], scores, -1e+30), axis=2))
        weights = jnp.exp(jnp.where(same_doc[None], scores - row_max[:, :, None], -1e+30))
        totals = lax.optimization_barrier(jnp.sum(weights, axis=2))
        rounded = weights.astype(jnp.bfloat16).astype(jnp.float32)
        partial_value = jnp.einsum('hqk,khd->qhd', rounded, value_heads)
        return (partial_value.reshape(row_count, head_count * HD), row_max, totals)

    def dead_tile():
        return (jnp.zeros((row_count, head_count * HD), jnp.float32), jnp.full((head_count, row_count), -1e+30, jnp.float32), jnp.zeros((head_count, row_count), jnp.float32))
    return lax.cond(jnp.any(same_doc), live_tile, dead_tile)

def merge_partials(partials):
    overall = partials[0][1]
    for entry in partials[1:]:
        overall = jnp.maximum(overall, entry[1])
    row_count = partials[0][0].shape[0]
    head_count = overall.shape[0]
    numerator = jnp.zeros((row_count, head_count, HD), jnp.float32)
    denominator = jnp.zeros((head_count, row_count), jnp.float32)
    for partial_value, tile_max, totals in partials:
        factor = jnp.exp(tile_max - overall)
        denominator = denominator + factor * totals
        numerator = numerator + partial_value.reshape(row_count, head_count, HD) * jnp.transpose(factor)[:, :, None]
    result = numerator / jnp.transpose(denominator)[:, :, None]
    return result.reshape(row_count, head_count * HD).astype(jnp.bfloat16)

def reference(queries, keys, values, doc_ids):
    block_count = SEQ // BLK

    def one_block(block_index):
        row_start = (block_index * BLK).astype(jnp.int32)
        query_rows = lax.dynamic_slice_in_dim(queries, row_start, BLK, 0)
        own_ids = lax.dynamic_slice_in_dim(doc_ids, row_start, BLK, 0)
        partials = []
        for offset in range(-SPAN, SPAN + 1):
            neighbour = block_index + offset
            inside = (neighbour >= 0) & (neighbour < block_count)
            clipped = (jnp.clip(neighbour, 0, block_count - 1) * BLK).astype(jnp.int32)
            key_rows = lax.dynamic_slice_in_dim(keys, clipped, BLK, 0)
            value_rows = lax.dynamic_slice_in_dim(values, clipped, BLK, 0)
            key_ids = jnp.where(inside, lax.dynamic_slice_in_dim(doc_ids, clipped, BLK, 0), -1)
            partials.append(score_tiles(query_rows, key_rows, value_rows, own_ids, key_ids))
        return merge_partials(partials)
    blocks = lax.map(one_block, jnp.arange(block_count, dtype=jnp.int32))
    return blocks.reshape(SEQ, FEAT)
```

```python
import math

import jax
import jax.numpy as jnp
from jax import lax
from jax.experimental import pallas as pl
from jax.experimental.pallas import tpu as pltpu
from jax.sharding import PartitionSpec as P

HD = 128
ROWS = 128
PARTS = 8
HEADS = 2
WIDE = HEADS * HD
TAGS = 16
PIECE = 2 * ROWS + TAGS
BLOCK = PARTS * ROWS
TILE = 2 * ROWS
TILES = BLOCK // TILE
BIG = 1e30
EXP2_SCALE = math.log2(math.e) / math.sqrt(HD)
HBM = pl.BlockSpec(memory_space=pltpu.HBM)
ANY = pl.BlockSpec(memory_space=pl.ANY)
SMEM = pl.BlockSpec(memory_space=pltpu.SMEM)
VMEM = pl.BlockSpec(memory_space=pltpu.VMEM)
LIMIT = pltpu.CompilerParams(vmem_limit_bytes=32 * 1024 * 1024)
F32 = jnp.float32
BF16 = jnp.bfloat16


def estimate(work):
    return pl.CostEstimate(flops=work << 30, bytes_accessed=work << 21, transcendentals=0)


def run_copies(pairs, sems):
    copies = [pltpu.make_async_copy(s, t, sems.at[i]) for i, (s, t) in enumerate(pairs)]
    for copy in copies:
        copy.start()
    return copies


def head_cols(h):
    return slice(h * HD, (h + 1) * HD)


def part_cols(p):
    return slice(p * WIDE, (p + 1) * WIDE)


def pack_kv_kernel(ids, keys, values, kv, sems):
    pairs = []
    for p in range(PARTS):
        pairs += [
            (keys.at[:, part_cols(p)], kv.at[p, 0:ROWS]),
            (values.at[:, part_cols(p)], kv.at[p, ROWS : 2 * ROWS]),
        ]
    copies = run_copies(pairs, sems)
    row = jnp.broadcast_to(ids[...].astype(F32), (TAGS, ROWS))
    tags = jnp.concatenate([row] * HEADS, axis=1).astype(BF16)
    for p in range(PARTS):
        kv[p, 2 * ROWS : PIECE, :] = tags
    for copy in copies:
        copy.wait()


def pack_kv(ids, keys, values):
    return pl.pallas_call(
        pack_kv_kernel,
        out_shape=jax.ShapeDtypeStruct((PARTS, PIECE, WIDE), BF16),
        in_specs=[VMEM, HBM, HBM],
        out_specs=VMEM,
        scratch_shapes=[pltpu.SemaphoreType.DMA((2 * PARTS,))],
        compiler_params=pltpu.CompilerParams(vmem_limit_bytes=61 * 1024 * 1024),
        name="pack_kv",
    )(ids, keys, values)


def pack_q_kernel(queries, qs, sems):
    copies = run_copies(
        [(queries.at[:, part_cols(p)], qs.at[p]) for p in range(PARTS)], sems
    )
    for copy in copies:
        copy.wait()


def pack_q(queries):
    return pl.pallas_call(
        pack_q_kernel,
        out_shape=jax.ShapeDtypeStruct((PARTS, ROWS, WIDE), BF16),
        in_specs=[HBM],
        out_specs=VMEM,
        scratch_shapes=[pltpu.SemaphoreType.DMA((PARTS,))],
        compiler_params=pltpu.CompilerParams(vmem_limit_bytes=61 * 1024 * 1024),
        cost_estimate=estimate(8),
        name="pack_q",
    )(queries)


def unpack_kernel(parts, out, sems):
    copies = run_copies([(parts.at[p], out.at[:, part_cols(p)]) for p in range(PARTS)], sems)
    for copy in copies:
        copy.wait()


def unpack(parts):
    return pl.pallas_call(
        unpack_kernel,
        out_shape=jax.ShapeDtypeStruct((ROWS, PARTS * WIDE), BF16),
        in_specs=[VMEM],
        out_specs=HBM,
        scratch_shapes=[pltpu.SemaphoreType.DMA((PARTS,))],
        compiler_params=LIMIT,
        name="unpack",
    )(parts)


def id_row(ref, p):
    return ref[p, 2 * ROWS : PIECE, 0:ROWS].astype(F32)[0:1, :]


def down_rows(row):
    return jnp.transpose(jnp.broadcast_to(row, (ROWS, ROWS)))


def tile_ids(ref, tile):
    return jnp.concatenate([id_row(ref, 2 * tile), id_row(ref, 2 * tile + 1)], axis=1)


def tile_rows(ref, tile, part, h):
    rows = slice(part * ROWS, (part + 1) * ROWS)
    return jnp.concatenate([ref[2 * tile + i, rows, head_cols(h)] for i in range(2)], axis=0)


def query_rows(ref, tile, h):
    return jnp.concatenate([ref[2 * tile + i, :, head_cols(h)] for i in range(2)], axis=0)


def scores_of(q, k):
    return lax.dot_general(q, k, (((1,), (1,)), ((), ())), preferred_element_type=F32)


def weigh(weights, v):
    ones = jnp.ones((v.shape[0], HD), BF16)
    return jnp.dot(
        weights.astype(BF16), jnp.concatenate([v, ones], axis=1), preferred_element_type=F32
    )


def wide(value):
    return jnp.concatenate([value, value], axis=1)


def own_kernel(kv, qs, q_ids, out_sum, out_total, out_max, scores):
    for p in range(PARTS):
        q_ids[p * ROWS : (p + 1) * ROWS, :] = down_rows(id_row(kv, p))
    for t in range(TILES):
        rows = slice(t * TILE, (t + 1) * TILE)
        tops = [None] * HEADS
        for k in range(TILES):
            same = wide(q_ids[rows, :]) == tile_ids(kv, k)
            bias = jnp.where(same, 0.0, -BIG)
            for h in range(HEADS):
                part = scores_of(query_rows(qs, t, h), tile_rows(kv, k, 0, h)) + bias
                scores[h, :, k * TILE : (k + 1) * TILE] = part
                best = jnp.maximum(part[:, :HD], part[:, HD:])
                tops[h] = best if k == 0 else jnp.maximum(tops[h], best)
        for h in range(HEADS):
            top = jnp.broadcast_to(jnp.max(tops[h], axis=1, keepdims=True), (TILE, HD))
            both = None
            for k in range(TILES):
                part = scores[h, :, k * TILE : (k + 1) * TILE]
                weights = jnp.exp2((part - wide(top)) * EXP2_SCALE)
                added = weigh(weights, tile_rows(kv, k, 1, h))
                both = added if k == 0 else both + added
            out_sum[rows, head_cols(h)] = both[:, :HD]
            out_total[rows, head_cols(h)] = both[:, HD:]
            out_max[rows, head_cols(h)] = top


def own_block(kv, qs):
    state = jax.ShapeDtypeStruct((BLOCK, WIDE), F32)
    return pl.pallas_call(
        own_kernel,
        out_shape=[jax.ShapeDtypeStruct((BLOCK, ROWS), F32), state, state, state],
        in_specs=[VMEM] * 2,
        out_specs=[VMEM] * 4,
        scratch_shapes=[pltpu.VMEM((HEADS, TILE, BLOCK), F32)],
        compiler_params=LIMIT,
        cost_estimate=estimate(8),
        name="own_block",
    )(kv, qs)


def near_kernel(place, up, down, qs, q_ids, own_sum, own_total, own_max, out, sum_, total, top_):
    sum_[...] = jnp.zeros_like(sum_)
    total[...] = jnp.zeros_like(total)
    top_[...] = jnp.full_like(top_, -BIG)
    lows = [jnp.max(q_ids[t * TILE : t * TILE + 1, :]) for t in range(TILES)]
    highs = [jnp.max(q_ids[(t + 1) * TILE - 1 : (t + 1) * TILE, :]) for t in range(TILES)]
    ids = [[tile_ids(ref, k) for k in range(TILES)] for ref in (up, down)]
    lasts = [jnp.max(row) for row in ids[0]]
    firsts = [jnp.min(row) for row in ids[1]]
    for side, ref in enumerate((up, down)):
        for k in range(TILES):
            k_ids = ids[side][k]
            for t in range(TILES):
                rows = slice(t * TILE, (t + 1) * TILE)
                if side:
                    live = (firsts[k] <= highs[t]) & (place[0] < place[1] - 1)
                else:
                    live = (lasts[k] >= lows[t]) & (place[0] > 0)

                @pl.when(live)
                def _(ref=ref, k=k, t=t, rows=rows, k_ids=k_ids):
                    bias = jnp.where(wide(q_ids[rows, :]) == k_ids, 0.0, -BIG)
                    for h in range(HEADS):
                        cols = head_cols(h)
                        scores = scores_of(query_rows(qs, t, h), tile_rows(ref, k, 0, h)) + bias
                        old = top_[rows, cols]
                        new = jnp.maximum(old, jnp.max(scores, axis=1, keepdims=True))
                        factor = jnp.exp2((old - new) * EXP2_SCALE)
                        weights = jnp.exp2((scores - wide(new)) * EXP2_SCALE)
                        both = weigh(weights, tile_rows(ref, k, 1, h))
                        sum_[rows, cols] = sum_[rows, cols] * factor + both[:, :HD]
                        total[rows, cols] = total[rows, cols] * factor + both[:, HD:]
                        top_[rows, cols] = new

    for p in range(PARTS):
        rows = slice(p * ROWS, (p + 1) * ROWS)
        best = jnp.maximum(top_[rows, :], own_max[rows, :])
        far = jnp.exp2((top_[rows, :] - best) * EXP2_SCALE)
        near = jnp.exp2((own_max[rows, :] - best) * EXP2_SCALE)
        value = near * own_sum[rows, :] + far * sum_[rows, :]
        scale = near * own_total[rows, :] + far * total[rows, :]
        out[p] = (value / scale).astype(BF16)


def near_blocks(place, up, down, qs, state):
    return pl.pallas_call(
        near_kernel,
        out_shape=jax.ShapeDtypeStruct((PARTS, ROWS, WIDE), BF16),
        in_specs=[SMEM] + [VMEM] * 7,
        out_specs=VMEM,
        scratch_shapes=[pltpu.VMEM((BLOCK, WIDE), F32)] * 3,
        compiler_params=LIMIT,
        cost_estimate=estimate(3),
        name="near_blocks",
    )(place, up, down, qs, *state)


def across_heads(value):
    return lax.all_to_all(value, "head", 0, 0, tiled=True)


def across_blocks(value, step):
    size = lax.axis_size("seq")
    return lax.ppermute(value, "seq", [(i, (i + step) % size) for i in range(size)])


def per_device(queries, keys, values, doc_ids):
    count = jnp.int32(lax.axis_size("seq"))
    place = jnp.stack([lax.axis_index("seq"), count]).astype(jnp.int32)
    kv = across_heads(pack_kv(doc_ids.reshape(1, ROWS), keys, values))
    kv, queries = lax.optimization_barrier((kv, queries))
    up, down = across_blocks(kv, 1), across_blocks(kv, -1)
    qs = across_heads(pack_q(queries))
    state = own_block(kv, qs)
    out = near_blocks(place, up, down, qs, state)
    return unpack(across_heads(out))


def solution(mesh):
    return jax.shard_map(
        per_device,
        mesh=mesh,
        in_specs=(
            P(("seq", "head"), None),
            P(("seq", "head"), None),
            P(("seq", "head"), None),
            P(("seq", "head")),
        ),
        out_specs=P(("seq", "head"), None),
        check_vma=False,
    )
```

```python
import functools
import math

import jax
import jax.numpy as jnp
from jax import lax
from jax.experimental import pallas as pl
from jax.experimental.pallas import tpu as pltpu
from jax.sharding import PartitionSpec as P

HD = 128
ROWS = 128
PARTS = 8
HEADS = 2
WIDE = HEADS * HD
TAGS = 16
PIECE = 2 * ROWS + TAGS
BLOCK = PARTS * ROWS
TILE = 2 * ROWS
TILES = BLOCK // TILE
SPAN = 2
BIG = 1e30
HEADROOM = 60.0
EXP2_SCALE = math.log2(math.e) / math.sqrt(HD)
HBM = pl.BlockSpec(memory_space=pltpu.HBM)
ANY = pl.BlockSpec(memory_space=pl.ANY)
SMEM = pl.BlockSpec(memory_space=pltpu.SMEM)
VMEM = pl.BlockSpec(memory_space=pltpu.VMEM)
LIMIT = pltpu.CompilerParams(vmem_limit_bytes=32 * 1024 * 1024)
F32 = jnp.float32
BF16 = jnp.bfloat16


def estimate(work):
    return pl.CostEstimate(flops=work << 30, bytes_accessed=work << 21, transcendentals=0)


def run_copies(pairs, sems):
    copies = [pltpu.make_async_copy(s, t, sems.at[i]) for i, (s, t) in enumerate(pairs)]
    for copy in copies:
        copy.start()
    return copies


def head_cols(h):
    return slice(h * HD, (h + 1) * HD)


def part_cols(p):
    return slice(p * WIDE, (p + 1) * WIDE)


def pack_kv_kernel(ids, keys, values, kv, sems):
    pairs = []
    for p in range(PARTS):
        pairs += [
            (keys.at[:, part_cols(p)], kv.at[p, 0:ROWS]),
            (values.at[:, part_cols(p)], kv.at[p, ROWS : 2 * ROWS]),
        ]
    copies = run_copies(pairs, sems)
    row = jnp.broadcast_to(ids[...].astype(F32), (TAGS, ROWS))
    tags = jnp.concatenate([row] * HEADS, axis=1).astype(BF16)
    for p in range(PARTS):
        kv[p, 2 * ROWS : PIECE, :] = tags
    for copy in copies:
        copy.wait()


def pack_kv(ids, keys, values):
    return pl.pallas_call(
        pack_kv_kernel,
        out_shape=jax.ShapeDtypeStruct((PARTS, PIECE, WIDE), BF16),
        in_specs=[VMEM, HBM, HBM],
        out_specs=VMEM,
        scratch_shapes=[pltpu.SemaphoreType.DMA((2 * PARTS,))],
        compiler_params=pltpu.CompilerParams(vmem_limit_bytes=61 * 1024 * 1024),
        name="pack_kv",
    )(ids, keys, values)


def pack_q_kernel(queries, qs, sems):
    copies = run_copies(
        [(queries.at[:, part_cols(p)], qs.at[p]) for p in range(PARTS)], sems
    )
    for copy in copies:
        copy.wait()


def pack_q(queries):
    return pl.pallas_call(
        pack_q_kernel,
        out_shape=jax.ShapeDtypeStruct((PARTS, ROWS, WIDE), BF16),
        in_specs=[HBM],
        out_specs=VMEM,
        scratch_shapes=[pltpu.SemaphoreType.DMA((PARTS,))],
        compiler_params=LIMIT,
        cost_estimate=estimate(0),
        name="pack_q",
    )(queries)


def unpack_kernel(parts, out, sems):
    copies = run_copies([(parts.at[p], out.at[:, part_cols(p)]) for p in range(PARTS)], sems)
    for copy in copies:
        copy.wait()


def unpack(parts):
    return pl.pallas_call(
        unpack_kernel,
        out_shape=jax.ShapeDtypeStruct((ROWS, PARTS * WIDE), BF16),
        in_specs=[VMEM],
        out_specs=HBM,
        scratch_shapes=[pltpu.SemaphoreType.DMA((PARTS,))],
        compiler_params=LIMIT,
        name="unpack",
    )(parts)


def id_row(ref, p):
    return ref[p, 2 * ROWS : PIECE, 0:ROWS].astype(F32)[0:1, :]


def down_rows(row):
    return jnp.transpose(jnp.broadcast_to(row, (ROWS, ROWS)))


def tile_ids(ref, tile):
    return jnp.concatenate([id_row(ref, 2 * tile), id_row(ref, 2 * tile + 1)], axis=1)


def tile_rows(ref, tile, part, h):
    rows = slice(part * ROWS, (part + 1) * ROWS)
    return jnp.concatenate([ref[2 * tile + i, rows, head_cols(h)] for i in range(2)], axis=0)


def query_rows(ref, tile, h):
    return jnp.concatenate([ref[2 * tile + i, :, head_cols(h)] for i in range(2)], axis=0)


def scores_of(q, k):
    return lax.dot_general(q, k, (((1,), (1,)), ((), ())), preferred_element_type=F32)


def weigh(weights, v):
    ones = jnp.ones((v.shape[0], HD), BF16)
    return jnp.dot(
        weights.astype(BF16), jnp.concatenate([v, ones], axis=1), preferred_element_type=F32
    )


def wide(value):
    return jnp.concatenate([value, value], axis=1)


def own_kernel(kv, qs, q_ids, out_sum, out_total, out_max, scores):
    for p in range(PARTS):
        q_ids[p * ROWS : (p + 1) * ROWS, :] = down_rows(id_row(kv, p))
    for t in range(TILES):
        rows = slice(t * TILE, (t + 1) * TILE)
        tops = [None] * HEADS
        for k in range(TILES):
            same = wide(q_ids[rows, :]) == tile_ids(kv, k)
            bias = jnp.where(same, 0.0, -BIG)
            for h in range(HEADS):
                part = scores_of(query_rows(qs, t, h), tile_rows(kv, k, 0, h)) + bias
                scores[h, :, k * TILE : (k + 1) * TILE] = part
                best = jnp.maximum(part[:, :HD], part[:, HD:])
                tops[h] = best if k == 0 else jnp.maximum(tops[h], best)
        for h in range(HEADS):
            top = jnp.broadcast_to(jnp.max(tops[h], axis=1, keepdims=True), (TILE, HD))
            both = None
            for k in range(TILES):
                part = scores[h, :, k * TILE : (k + 1) * TILE]
                weights = jnp.exp2((part - wide(top)) * EXP2_SCALE)
                added = weigh(weights, tile_rows(kv, k, 1, h))
                both = added if k == 0 else both + added
            out_sum[rows, head_cols(h)] = both[:, :HD]
            out_total[rows, head_cols(h)] = both[:, HD:]
            out_max[rows, head_cols(h)] = top


def own_block(kv, qs):
    state = jax.ShapeDtypeStruct((BLOCK, WIDE), F32)
    return pl.pallas_call(
        own_kernel,
        out_shape=[jax.ShapeDtypeStruct((BLOCK, ROWS), F32), state, state, state],
        in_specs=[VMEM] * 2,
        out_specs=[VMEM] * 4,
        scratch_shapes=[pltpu.VMEM((HEADS, TILE, BLOCK), F32)],
        compiler_params=LIMIT,
        cost_estimate=estimate(0),
        name="own_block",
    )(kv, qs)


def span_rows(ref, k, part, h):
    return jnp.concatenate([tile_rows(ref, k * SPAN + i, part, h) for i in range(SPAN)], axis=0)


def spread(value, count):
    return jnp.concatenate([value] * count, axis=1)


def near_kernel(final, ref, qs, q_ids, sum_in, total_in, max_in, *rest):
    if final:
        ready, out, sums, totals, tops, excess = rest
    else:
        sums, totals, tops, out, excess = rest
    spans = range(TILES // SPAN)
    lows = [jnp.max(q_ids[t * TILE : t * TILE + 1, :]) for t in range(TILES)]
    highs = [jnp.max(q_ids[(t + 1) * TILE - 1 : (t + 1) * TILE, :]) for t in range(TILES)]
    ids = [
        jnp.concatenate([tile_ids(ref, k * SPAN + i) for i in range(SPAN)], axis=1) for k in spans
    ]
    firsts = [jnp.min(row) for row in ids]
    lasts = [jnp.max(row) for row in ids]
    excess[...] = jnp.full_like(excess, -BIG)
    lives = [
        [(firsts[k] <= highs[t]) & (lasts[k] >= lows[t]) for k in spans] for t in range(TILES)
    ]
    active = [functools.reduce(jnp.logical_or, lives[t]) for t in range(TILES)]

    def masked_scores(t, k, h, bias):
        return scores_of(query_rows(qs, t, h), span_rows(ref, k, 0, h)) + bias

    def bias_of(rows, k):
        return jnp.where(spread(q_ids[rows, :], 2 * SPAN) == ids[k], 0.0, -BIG)

    def best_of(part):
        return functools.reduce(
            jnp.maximum, [part[:, c * HD : (c + 1) * HD] for c in range(2 * SPAN)]
        )

    def copy_state(rows):
        sums[rows, :] = sum_in[rows, :]
        totals[rows, :] = total_in[rows, :]
        tops[rows, :] = max_in[rows, :]

    def finish(t, rows):
        result = (sums[rows, :] / totals[rows, :]).astype(BF16)
        for i in range(2):
            out[2 * t + i] = result[i * ROWS : (i + 1) * ROWS, :]

    for t in range(TILES):
        rows = slice(t * TILE, (t + 1) * TILE)
        if not final:
            copy_state(rows)

        @pl.when(active[t])
        def _(t=t, rows=rows):
            if final:
                copy_state(rows)
            for k in spans:

                @pl.when(lives[t][k])
                def _(k=k):
                    bias = bias_of(rows, k)
                    for h in range(HEADS):
                        cols = head_cols(h)
                        above = masked_scores(t, k, h, bias) - spread(max_in[rows, cols], 2 * SPAN)
                        excess[...] = jnp.maximum(excess[...], best_of(above))
                        both = weigh(jnp.exp2(above * EXP2_SCALE), span_rows(ref, k, 1, h))
                        sums[rows, cols] += both[:, :HD]
                        totals[rows, cols] += both[:, HD:]

    @pl.when(jnp.max(excess[...]) * EXP2_SCALE > HEADROOM)
    def _():
        for t in range(TILES):
            rows = slice(t * TILE, (t + 1) * TILE)

            @pl.when(active[t])
            def _(t=t, rows=rows):
                copy_state(rows)
                for k in spans:

                    @pl.when(lives[t][k])
                    def _(k=k):
                        bias = bias_of(rows, k)
                        for h in range(HEADS):
                            cols = head_cols(h)
                            part = masked_scores(t, k, h, bias)
                            old = tops[rows, cols]
                            new = jnp.max(best_of(part), axis=1, keepdims=True)
                            new = jnp.maximum(old, new)
                            factor = jnp.exp2((old - new) * EXP2_SCALE)
                            part = jnp.exp2((part - spread(new, 2 * SPAN)) * EXP2_SCALE)
                            both = weigh(part, span_rows(ref, k, 1, h))
                            sums[rows, cols] = sums[rows, cols] * factor + both[:, :HD]
                            totals[rows, cols] = totals[rows, cols] * factor + both[:, HD:]
                            tops[rows, cols] = new

    for t in range(TILES):
        rows = slice(t * TILE, (t + 1) * TILE)
        if final:
            pl.when(active[t])(functools.partial(finish, t, rows))

            @pl.when(jnp.logical_not(active[t]))
            def _(t=t):
                for i in range(2):
                    out[2 * t + i] = ready[2 * t + i]

        else:
            finish(t, rows)


def near_block(final, ref, qs, q_ids, state, *ready):
    state_shape = [jax.ShapeDtypeStruct((BLOCK, WIDE), F32)] * 3
    result = jax.ShapeDtypeStruct((PARTS, ROWS, WIDE), BF16)
    excess = pltpu.VMEM((TILE, HD), F32)
    work = [pltpu.VMEM((BLOCK, WIDE), F32)] * 3
    return pl.pallas_call(
        functools.partial(near_kernel, final),
        out_shape=result if final else state_shape + [result],
        in_specs=[VMEM] * (6 + len(ready)),
        out_specs=VMEM if final else [VMEM] * 4,
        scratch_shapes=work + [excess] if final else [excess],
        compiler_params=LIMIT,
        name="last_block" if final else "near_block",
    )(ref, qs, q_ids, *state, *ready)


def across_heads(value):
    return lax.all_to_all(value, "head", 0, 0, tiled=True)


def swapped(value, first):
    size = lax.axis_size("seq")
    pairs = []
    for i in range(first, size + first, 2):
        pairs += [(i % size, (i + 1) % size), ((i + 1) % size, i % size)]
    return lax.ppermute(value, "seq", pairs)


def per_device(queries, keys, values, doc_ids):
    kv = across_heads(pack_kv(doc_ids.reshape(1, ROWS), keys, values))
    kv, queries = lax.optimization_barrier((kv, queries))
    even, odd = swapped(kv, 0), swapped(kv, 1)
    qs = across_heads(pack_q(queries))
    q_ids, *state = own_block(kv, qs)
    *state, ready = near_block(False, odd, qs, q_ids, state)
    out = near_block(True, even, qs, q_ids, state, ready)
    return unpack(across_heads(out))


def solution(mesh):
    return jax.shard_map(
        per_device,
        mesh=mesh,
        in_specs=(
            P(("seq", "head"), None),
            P(("seq", "head"), None),
            P(("seq", "head"), None),
            P(("seq", "head")),
        ),
        out_specs=P(("seq", "head"), None),
        check_vma=False,
    )
```

```python
import functools
import math

import jax
import jax.numpy as jnp
from jax import lax
from jax.experimental import pallas as pl
from jax.experimental.pallas import tpu as pltpu
from jax.sharding import PartitionSpec as P

HD = 128
ROWS = 128
PARTS = 8
HEADS = 2
WIDE = HEADS * HD
TAGS = 16
PIECE = 2 * ROWS + TAGS
BLOCK = PARTS * ROWS
TILE = 2 * ROWS
TILES = BLOCK // TILE
SPAN = 2
BIG = 1e30
HEADROOM = 60.0
EXP2_SCALE = math.log2(math.e) / math.sqrt(HD)
HBM = pl.BlockSpec(memory_space=pltpu.HBM)
ANY = pl.BlockSpec(memory_space=pl.ANY)
SMEM = pl.BlockSpec(memory_space=pltpu.SMEM)
VMEM = pl.BlockSpec(memory_space=pltpu.VMEM)
LIMIT = pltpu.CompilerParams(vmem_limit_bytes=32 * 1024 * 1024)
F32 = jnp.float32
BF16 = jnp.bfloat16


def estimate(work):
    return pl.CostEstimate(flops=work << 30, bytes_accessed=work << 21, transcendentals=0)


def run_copies(pairs, sems):
    copies = [pltpu.make_async_copy(s, t, sems.at[i]) for i, (s, t) in enumerate(pairs)]
    for copy in copies:
        copy.start()
    return copies


def head_cols(h):
    return slice(h * HD, (h + 1) * HD)


def part_cols(p):
    return slice(p * WIDE, (p + 1) * WIDE)


def pack_kv_kernel(ids, keys, values, kv):
    row = jnp.broadcast_to(ids[...].astype(F32), (TAGS, ROWS))
    tags = jnp.concatenate([row] * HEADS, axis=1).astype(BF16)
    for p in range(PARTS):
        kv[p, 0:ROWS, :] = keys[:, part_cols(p)]
        kv[p, ROWS : 2 * ROWS, :] = values[:, part_cols(p)]
        kv[p, 2 * ROWS : PIECE, :] = tags


def pack_kv(ids, keys, values):
    return pl.pallas_call(
        pack_kv_kernel,
        out_shape=jax.ShapeDtypeStruct((PARTS, PIECE, WIDE), BF16),
        in_specs=[VMEM] * 3,
        out_specs=VMEM,
        compiler_params=LIMIT,
        name="pack_kv",
    )(ids, keys, values)


def gather_kernel(parts, kv):
    for p in range(PARTS):
        kv[p * ROWS : (p + 1) * ROWS, :] = parts[p, 0:ROWS, :]
        kv[BLOCK + p * ROWS : BLOCK + (p + 1) * ROWS, :] = parts[p, ROWS : 2 * ROWS, :]
    rows = [parts[p, 2 * ROWS : PIECE, :].astype(F32)[0:1, :] for p in range(PARTS)]
    kv[2 * BLOCK : 2 * BLOCK + TAGS, :] = jnp.concatenate(rows * 2, axis=0).astype(BF16)


def gather(parts):
    return pl.pallas_call(
        gather_kernel,
        out_shape=jax.ShapeDtypeStruct((2 * BLOCK + TAGS, WIDE), BF16),
        in_specs=[VMEM],
        out_specs=VMEM,
        compiler_params=LIMIT,
        name="gather",
    )(parts)


def pack_q_kernel(queries, qs, sems):
    copies = run_copies(
        [(queries.at[:, part_cols(p)], qs.at[p]) for p in range(PARTS)], sems
    )
    for copy in copies:
        copy.wait()


def pack_q(queries):
    return pl.pallas_call(
        pack_q_kernel,
        out_shape=jax.ShapeDtypeStruct((PARTS, ROWS, WIDE), BF16),
        in_specs=[HBM],
        out_specs=VMEM,
        scratch_shapes=[pltpu.SemaphoreType.DMA((PARTS,))],
        compiler_params=LIMIT,
        cost_estimate=estimate(0),
        name="pack_q",
    )(queries)


def unpack_kernel(parts, out, sems):
    copies = run_copies([(parts.at[p], out.at[:, part_cols(p)]) for p in range(PARTS)], sems)
    for copy in copies:
        copy.wait()


def unpack(parts):
    return pl.pallas_call(
        unpack_kernel,
        out_shape=jax.ShapeDtypeStruct((ROWS, PARTS * WIDE), BF16),
        in_specs=[VMEM],
        out_specs=HBM,
        scratch_shapes=[pltpu.SemaphoreType.DMA((PARTS,))],
        compiler_params=LIMIT,
        name="unpack",
    )(parts)


def id_row(ref, p):
    return ref[2 * BLOCK : 2 * BLOCK + TAGS, 0:ROWS].astype(F32)[p : p + 1, :]


def down_rows(row):
    return jnp.transpose(jnp.broadcast_to(row, (ROWS, ROWS)))


def tile_ids(ref, tile):
    return jnp.concatenate([id_row(ref, 2 * tile), id_row(ref, 2 * tile + 1)], axis=1)


def tile_rows(ref, tile, part, h, count=1):
    base = part * BLOCK + tile * TILE
    return ref[base : base + count * TILE, head_cols(h)]


def query_rows(ref, tile, h):
    return jnp.concatenate([ref[2 * tile + i, :, head_cols(h)] for i in range(2)], axis=0)


def scores_of(q, k):
    return lax.dot_general(q, k, (((1,), (1,)), ((), ())), preferred_element_type=F32)


def weigh(weights, v):
    ones = jnp.ones((v.shape[0], HD), BF16)
    return jnp.dot(
        weights.astype(BF16), jnp.concatenate([v, ones], axis=1), preferred_element_type=F32
    )


def wide(value):
    return jnp.concatenate([value, value], axis=1)


def own_kernel(kv, qs, q_ids, out_sum, out_total, out_max, scores):
    for p in range(PARTS):
        q_ids[p * ROWS : (p + 1) * ROWS, :] = down_rows(id_row(kv, p))
    for t in range(TILES):
        rows = slice(t * TILE, (t + 1) * TILE)
        tops = [None] * HEADS
        for k in range(TILES):
            same = wide(q_ids[rows, :]) == tile_ids(kv, k)
            bias = jnp.where(same, 0.0, -BIG)
            for h in range(HEADS):
                part = scores_of(query_rows(qs, t, h), tile_rows(kv, k, 0, h)) + bias
                scores[h, :, k * TILE : (k + 1) * TILE] = part
                best = jnp.maximum(part[:, :HD], part[:, HD:])
                tops[h] = best if k == 0 else jnp.maximum(tops[h], best)
        for h in range(HEADS):
            top = jnp.broadcast_to(jnp.max(tops[h], axis=1, keepdims=True), (TILE, HD))
            both = None
            for k in range(TILES):
                part = scores[h, :, k * TILE : (k + 1) * TILE]
                weights = jnp.exp2((part - wide(top)) * EXP2_SCALE)
                added = weigh(weights, tile_rows(kv, k, 1, h))
                both = added if k == 0 else both + added
            out_sum[rows, head_cols(h)] = both[:, :HD]
            out_total[rows, head_cols(h)] = both[:, HD:]
            out_max[rows, head_cols(h)] = top


def own_block(kv, qs):
    state = jax.ShapeDtypeStruct((BLOCK, WIDE), F32)
    return pl.pallas_call(
        own_kernel,
        out_shape=[jax.ShapeDtypeStruct((BLOCK, ROWS), F32), state, state, state],
        in_specs=[VMEM] * 2,
        out_specs=[VMEM] * 4,
        scratch_shapes=[pltpu.VMEM((HEADS, TILE, BLOCK), F32)],
        compiler_params=LIMIT,
        cost_estimate=estimate(0),
        name="own_block",
    )(kv, qs)


def span_rows(ref, k, part, h):
    return tile_rows(ref, k * SPAN, part, h, SPAN)


def spread(value, count):
    return jnp.concatenate([value] * count, axis=1)


def near_kernel(final, ref, qs, q_ids, sum_in, total_in, max_in, *rest):
    if final:
        ready, out, sums, totals, tops, excess = rest
    else:
        sums, totals, tops, out, excess = rest
    spans = range(TILES // SPAN)
    lows = [jnp.max(q_ids[t * TILE : t * TILE + 1, :]) for t in range(TILES)]
    highs = [jnp.max(q_ids[(t + 1) * TILE - 1 : (t + 1) * TILE, :]) for t in range(TILES)]
    ids = [
        jnp.concatenate([tile_ids(ref, k * SPAN + i) for i in range(SPAN)], axis=1) for k in spans
    ]
    firsts = [jnp.min(row) for row in ids]
    lasts = [jnp.max(row) for row in ids]
    excess[...] = jnp.full_like(excess, -BIG)
    lives = [
        [(firsts[k] <= highs[t]) & (lasts[k] >= lows[t]) for k in spans] for t in range(TILES)
    ]
    active = [functools.reduce(jnp.logical_or, lives[t]) for t in range(TILES)]

    def masked_scores(t, k, h, bias):
        return scores_of(query_rows(qs, t, h), span_rows(ref, k, 0, h)) + bias

    def bias_of(rows, k):
        return jnp.where(spread(q_ids[rows, :], 2 * SPAN) == ids[k], 0.0, -BIG)

    def best_of(part):
        return functools.reduce(
            jnp.maximum, [part[:, c * HD : (c + 1) * HD] for c in range(2 * SPAN)]
        )

    def copy_state(rows):
        sums[rows, :] = sum_in[rows, :]
        totals[rows, :] = total_in[rows, :]
        tops[rows, :] = max_in[rows, :]

    def finish(t, rows):
        result = (sums[rows, :] / totals[rows, :]).astype(BF16)
        for i in range(2):
            out[2 * t + i] = result[i * ROWS : (i + 1) * ROWS, :]

    for t in range(TILES):
        rows = slice(t * TILE, (t + 1) * TILE)
        if not final:
            copy_state(rows)

        @pl.when(active[t])
        def _(t=t, rows=rows):
            if final:
                copy_state(rows)
            for k in spans:

                @pl.when(lives[t][k])
                def _(k=k):
                    bias = bias_of(rows, k)
                    for h in range(HEADS):
                        cols = head_cols(h)
                        above = masked_scores(t, k, h, bias) - spread(max_in[rows, cols], 2 * SPAN)
                        excess[...] = jnp.maximum(excess[...], best_of(above))
                        both = weigh(jnp.exp2(above * EXP2_SCALE), span_rows(ref, k, 1, h))
                        sums[rows, cols] += both[:, :HD]
                        totals[rows, cols] += both[:, HD:]

    @pl.when(jnp.max(excess[...]) * EXP2_SCALE > HEADROOM)
    def _():
        for t in range(TILES):
            rows = slice(t * TILE, (t + 1) * TILE)

            @pl.when(active[t])
            def _(t=t, rows=rows):
                copy_state(rows)
                for k in spans:

                    @pl.when(lives[t][k])
                    def _(k=k):
                        bias = bias_of(rows, k)
                        for h in range(HEADS):
                            cols = head_cols(h)
                            part = masked_scores(t, k, h, bias)
                            old = tops[rows, cols]
                            new = jnp.max(best_of(part), axis=1, keepdims=True)
                            new = jnp.maximum(old, new)
                            factor = jnp.exp2((old - new) * EXP2_SCALE)
                            part = jnp.exp2((part - spread(new, 2 * SPAN)) * EXP2_SCALE)
                            both = weigh(part, span_rows(ref, k, 1, h))
                            sums[rows, cols] = sums[rows, cols] * factor + both[:, :HD]
                            totals[rows, cols] = totals[rows, cols] * factor + both[:, HD:]
                            tops[rows, cols] = new

    for t in range(TILES):
        rows = slice(t * TILE, (t + 1) * TILE)
        if final:
            pl.when(active[t])(functools.partial(finish, t, rows))

            @pl.when(jnp.logical_not(active[t]))
            def _(t=t):
                for i in range(2):
                    out[2 * t + i] = ready[2 * t + i]

        else:
            finish(t, rows)


def near_block(final, ref, qs, q_ids, state, *ready):
    state_shape = [jax.ShapeDtypeStruct((BLOCK, WIDE), F32)] * 3
    result = jax.ShapeDtypeStruct((PARTS, ROWS, WIDE), BF16)
    excess = pltpu.VMEM((TILE, HD), F32)
    work = [pltpu.VMEM((BLOCK, WIDE), F32)] * 3
    return pl.pallas_call(
        functools.partial(near_kernel, final),
        out_shape=result if final else state_shape + [result],
        in_specs=[VMEM] * (6 + len(ready)),
        out_specs=VMEM if final else [VMEM] * 4,
        scratch_shapes=work + [excess] if final else [excess],
        compiler_params=LIMIT,
        name="last_block" if final else "near_block",
    )(ref, qs, q_ids, *state, *ready)


def across_heads(value):
    return lax.all_to_all(value, "head", 0, 0, tiled=True)


def swapped(value, first):
    size = lax.axis_size("seq")
    pairs = []
    for i in range(first, size + first, 2):
        pairs += [(i % size, (i + 1) % size), ((i + 1) % size, i % size)]
    return lax.ppermute(value, "seq", pairs)


def per_device(queries, keys, values, doc_ids):
    kv = gather(across_heads(pack_kv(doc_ids.reshape(1, ROWS), keys, values)))
    kv, queries = lax.optimization_barrier((kv, queries))
    even, odd = swapped(kv, 0), swapped(kv, 1)
    qs = across_heads(pack_q(queries))
    q_ids, *state = own_block(kv, qs)
    *state, ready = near_block(False, even, qs, q_ids, state)
    out = near_block(True, odd, qs, q_ids, state, ready)
    return unpack(across_heads(out))


def solution(mesh):
    return jax.shard_map(
        per_device,
        mesh=mesh,
        in_specs=(
            P(("seq", "head"), None),
            P(("seq", "head"), None),
            P(("seq", "head"), None),
            P(("seq", "head")),
        ),
        out_specs=P(("seq", "head"), None),
        check_vma=False,
    )
```

```python
import functools
import math

import jax
import jax.numpy as jnp
from jax import lax
from jax.experimental import pallas as pl
from jax.experimental.pallas import tpu as pltpu
from jax.sharding import PartitionSpec as P

HD = 128
ROWS = 128
PARTS = 8
HEADS = 2
WIDE = HEADS * HD
TAGS = 16
PIECE = 2 * ROWS + TAGS
BLOCK = PARTS * ROWS
TILE = 2 * ROWS
TILES = BLOCK // TILE
SPAN = 2
BIG = 1e30
HEADROOM = 60.0
EXP2_SCALE = math.log2(math.e) / math.sqrt(HD)
HBM = pl.BlockSpec(memory_space=pltpu.HBM)
ANY = pl.BlockSpec(memory_space=pl.ANY)
SMEM = pl.BlockSpec(memory_space=pltpu.SMEM)
VMEM = pl.BlockSpec(memory_space=pltpu.VMEM)
LIMIT = pltpu.CompilerParams(vmem_limit_bytes=32 * 1024 * 1024)
F32 = jnp.float32
BF16 = jnp.bfloat16


def estimate(work):
    return pl.CostEstimate(flops=work << 30, bytes_accessed=work << 21, transcendentals=0)


def run_copies(pairs, sems):
    copies = [pltpu.make_async_copy(s, t, sems.at[i]) for i, (s, t) in enumerate(pairs)]
    for copy in copies:
        copy.start()
    return copies


def head_cols(h):
    return slice(h * HD, (h + 1) * HD)


def part_cols(p):
    return slice(p * WIDE, (p + 1) * WIDE)


def tag_kernel(ids, tags):
    lane = lax.broadcasted_iota(jnp.int32, (TAGS, ROWS), 1)
    row = jnp.zeros((TAGS, ROWS), jnp.int32)
    for i in range(ROWS):
        row = jnp.where(lane == i, ids[i], row)
    tags[...] = jnp.concatenate([row.astype(F32)] * HEADS, axis=1).astype(BF16)


def tag_rows(ids):
    return pl.pallas_call(
        tag_kernel,
        out_shape=jax.ShapeDtypeStruct((TAGS, WIDE), BF16),
        in_specs=[SMEM],
        out_specs=VMEM,
        compiler_params=LIMIT,
        cost_estimate=estimate(4),
        name="tag_rows",
    )(ids)


def pack_kv_kernel(tags, keys, values, kv):
    for p in range(PARTS):
        kv[p, 0:ROWS, :] = keys[:, part_cols(p)]
        kv[p, ROWS : 2 * ROWS, :] = values[:, part_cols(p)]
        kv[p, 2 * ROWS : PIECE, :] = tags[...]


def pack_kv(tags, keys, values):
    return pl.pallas_call(
        pack_kv_kernel,
        out_shape=jax.ShapeDtypeStruct((PARTS, PIECE, WIDE), BF16),
        in_specs=[VMEM] * 3,
        out_specs=VMEM,
        compiler_params=LIMIT,
        name="pack_kv",
    )(tags, keys, values)


def gather_kernel(parts, kv):
    for p in range(PARTS):
        kv[p * ROWS : (p + 1) * ROWS, :] = parts[p, 0:ROWS, :]
        kv[BLOCK + p * ROWS : BLOCK + (p + 1) * ROWS, :] = parts[p, ROWS : 2 * ROWS, :]
    rows = [parts[p, 2 * ROWS : PIECE, :].astype(F32)[0:1, :] for p in range(PARTS)]
    kv[2 * BLOCK : 2 * BLOCK + TAGS, :] = jnp.concatenate(rows * 2, axis=0).astype(BF16)


def gather(parts):
    return pl.pallas_call(
        gather_kernel,
        out_shape=jax.ShapeDtypeStruct((2 * BLOCK + TAGS, WIDE), BF16),
        in_specs=[VMEM],
        out_specs=VMEM,
        compiler_params=LIMIT,
        name="gather",
    )(parts)


def pack_q_kernel(queries, qs, sems):
    copies = run_copies(
        [(queries.at[:, part_cols(p)], qs.at[p]) for p in range(PARTS)], sems
    )
    for copy in copies:
        copy.wait()


def pack_q(queries):
    return pl.pallas_call(
        pack_q_kernel,
        out_shape=jax.ShapeDtypeStruct((PARTS, ROWS, WIDE), BF16),
        in_specs=[HBM],
        out_specs=VMEM,
        scratch_shapes=[pltpu.SemaphoreType.DMA((PARTS,))],
        compiler_params=LIMIT,
        cost_estimate=estimate(0),
        name="pack_q",
    )(queries)


def unpack_kernel(parts, out, sems):
    copies = run_copies([(parts.at[p], out.at[:, part_cols(p)]) for p in range(PARTS)], sems)
    for copy in copies:
        copy.wait()


def unpack(parts):
    return pl.pallas_call(
        unpack_kernel,
        out_shape=jax.ShapeDtypeStruct((ROWS, PARTS * WIDE), BF16),
        in_specs=[VMEM],
        out_specs=HBM,
        scratch_shapes=[pltpu.SemaphoreType.DMA((PARTS,))],
        compiler_params=LIMIT,
        name="unpack",
    )(parts)


def id_row(ref, p):
    return ref[2 * BLOCK : 2 * BLOCK + TAGS, 0:ROWS].astype(F32)[p : p + 1, :]


def down_rows(row):
    return jnp.transpose(jnp.broadcast_to(row, (ROWS, ROWS)))


def tile_ids(ref, tile):
    return jnp.concatenate([id_row(ref, 2 * tile), id_row(ref, 2 * tile + 1)], axis=1)


def tile_rows(ref, tile, part, h, count=1):
    base = part * BLOCK + tile * TILE
    return ref[base : base + count * TILE, head_cols(h)]


def query_rows(ref, tile, h):
    return jnp.concatenate([ref[2 * tile + i, :, head_cols(h)] for i in range(2)], axis=0)


def scores_of(q, k):
    return lax.dot_general(q, k, (((1,), (1,)), ((), ())), preferred_element_type=F32)


def weigh(weights, v):
    ones = jnp.ones((v.shape[0], HD), BF16)
    return jnp.dot(
        weights.astype(BF16), jnp.concatenate([v, ones], axis=1), preferred_element_type=F32
    )


def wide(value):
    return jnp.concatenate([value, value], axis=1)


def own_kernel(kv, qs, q_ids, out_sum, out_total, out_max, scores):
    for p in range(PARTS):
        q_ids[p * ROWS : (p + 1) * ROWS, :] = down_rows(id_row(kv, p))
    for t in range(TILES):
        rows = slice(t * TILE, (t + 1) * TILE)
        tops = [None] * HEADS
        for k in range(TILES):
            same = wide(q_ids[rows, :]) == tile_ids(kv, k)
            bias = jnp.where(same, 0.0, -BIG)
            for h in range(HEADS):
                part = scores_of(query_rows(qs, t, h), tile_rows(kv, k, 0, h)) + bias
                scores[h, :, k * TILE : (k + 1) * TILE] = part
                best = jnp.maximum(part[:, :HD], part[:, HD:])
                tops[h] = best if k == 0 else jnp.maximum(tops[h], best)
        for h in range(HEADS):
            top = jnp.broadcast_to(jnp.max(tops[h], axis=1, keepdims=True), (TILE, HD))
            both = None
            for k in range(TILES):
                part = scores[h, :, k * TILE : (k + 1) * TILE]
                weights = jnp.exp2((part - wide(top)) * EXP2_SCALE)
                added = weigh(weights, tile_rows(kv, k, 1, h))
                both = added if k == 0 else both + added
            out_sum[rows, head_cols(h)] = both[:, :HD]
            out_total[rows, head_cols(h)] = both[:, HD:]
            out_max[rows, head_cols(h)] = top


def own_block(kv, qs):
    state = jax.ShapeDtypeStruct((BLOCK, WIDE), F32)
    return pl.pallas_call(
        own_kernel,
        out_shape=[jax.ShapeDtypeStruct((BLOCK, ROWS), F32), state, state, state],
        in_specs=[VMEM] * 2,
        out_specs=[VMEM] * 4,
        scratch_shapes=[pltpu.VMEM((HEADS, TILE, BLOCK), F32)],
        compiler_params=LIMIT,
        cost_estimate=estimate(0),
        name="own_block",
    )(kv, qs)


def span_rows(ref, k, part, h):
    return tile_rows(ref, k * SPAN, part, h, SPAN)


def spread(value, count):
    return jnp.concatenate([value] * count, axis=1)


def near_kernel(final, ref, qs, q_ids, sum_in, total_in, max_in, *rest):
    if final:
        ready, out, sums, totals, tops, excess = rest
    else:
        sums, totals, tops, out, excess = rest
    spans = range(TILES // SPAN)
    lows = [jnp.max(q_ids[t * TILE : t * TILE + 1, :]) for t in range(TILES)]
    highs = [jnp.max(q_ids[(t + 1) * TILE - 1 : (t + 1) * TILE, :]) for t in range(TILES)]
    ids = [
        jnp.concatenate([tile_ids(ref, k * SPAN + i) for i in range(SPAN)], axis=1) for k in spans
    ]
    firsts = [jnp.min(row) for row in ids]
    lasts = [jnp.max(row) for row in ids]
    excess[...] = jnp.full_like(excess, -BIG)
    lives = [
        [(firsts[k] <= highs[t]) & (lasts[k] >= lows[t]) for k in spans] for t in range(TILES)
    ]
    active = [functools.reduce(jnp.logical_or, lives[t]) for t in range(TILES)]

    def masked_scores(t, k, h, bias):
        return scores_of(query_rows(qs, t, h), span_rows(ref, k, 0, h)) + bias

    def bias_of(rows, k):
        return jnp.where(spread(q_ids[rows, :], 2 * SPAN) == ids[k], 0.0, -BIG)

    def best_of(part):
        return functools.reduce(
            jnp.maximum, [part[:, c * HD : (c + 1) * HD] for c in range(2 * SPAN)]
        )

    def copy_state(rows):
        sums[rows, :] = sum_in[rows, :]
        totals[rows, :] = total_in[rows, :]
        tops[rows, :] = max_in[rows, :]

    def finish(t, rows):
        result = (sums[rows, :] / totals[rows, :]).astype(BF16)
        for i in range(2):
            out[2 * t + i] = result[i * ROWS : (i + 1) * ROWS, :]

    for t in range(TILES):
        rows = slice(t * TILE, (t + 1) * TILE)
        if not final:
            copy_state(rows)

        @pl.when(active[t])
        def _(t=t, rows=rows):
            if final:
                copy_state(rows)
            for k in spans:

                @pl.when(lives[t][k])
                def _(k=k):
                    bias = bias_of(rows, k)
                    for h in range(HEADS):
                        cols = head_cols(h)
                        above = masked_scores(t, k, h, bias) - spread(max_in[rows, cols], 2 * SPAN)
                        excess[...] = jnp.maximum(excess[...], best_of(above))
                        both = weigh(jnp.exp2(above * EXP2_SCALE), span_rows(ref, k, 1, h))
                        sums[rows, cols] += both[:, :HD]
                        totals[rows, cols] += both[:, HD:]

    @pl.when(jnp.max(excess[...]) * EXP2_SCALE > HEADROOM)
    def _():
        for t in range(TILES):
            rows = slice(t * TILE, (t + 1) * TILE)

            @pl.when(active[t])
            def _(t=t, rows=rows):
                copy_state(rows)
                for k in spans:

                    @pl.when(lives[t][k])
                    def _(k=k):
                        bias = bias_of(rows, k)
                        for h in range(HEADS):
                            cols = head_cols(h)
                            part = masked_scores(t, k, h, bias)
                            old = tops[rows, cols]
                            new = jnp.max(best_of(part), axis=1, keepdims=True)
                            new = jnp.maximum(old, new)
                            factor = jnp.exp2((old - new) * EXP2_SCALE)
                            part = jnp.exp2((part - spread(new, 2 * SPAN)) * EXP2_SCALE)
                            both = weigh(part, span_rows(ref, k, 1, h))
                            sums[rows, cols] = sums[rows, cols] * factor + both[:, :HD]
                            totals[rows, cols] = totals[rows, cols] * factor + both[:, HD:]
                            tops[rows, cols] = new

    for t in range(TILES):
        rows = slice(t * TILE, (t + 1) * TILE)
        if final:
            pl.when(active[t])(functools.partial(finish, t, rows))

            @pl.when(jnp.logical_not(active[t]))
            def _(t=t):
                for i in range(2):
                    out[2 * t + i] = ready[2 * t + i]

        else:
            finish(t, rows)


def near_block(final, ref, qs, q_ids, state, *ready):
    state_shape = [jax.ShapeDtypeStruct((BLOCK, WIDE), F32)] * 3
    result = jax.ShapeDtypeStruct((PARTS, ROWS, WIDE), BF16)
    excess = pltpu.VMEM((TILE, HD), F32)
    work = [pltpu.VMEM((BLOCK, WIDE), F32)] * 3
    return pl.pallas_call(
        functools.partial(near_kernel, final),
        out_shape=result if final else state_shape + [result],
        in_specs=[VMEM] * (6 + len(ready)),
        out_specs=VMEM if final else [VMEM] * 4,
        scratch_shapes=work + [excess] if final else [excess],
        compiler_params=LIMIT,
        name="last_block" if final else "near_block",
    )(ref, qs, q_ids, *state, *ready)


def across_heads(value):
    return lax.all_to_all(value, "head", 0, 0, tiled=True)


def swapped(value, first):
    size = lax.axis_size("seq")
    pairs = []
    for i in range(first, size + first, 2):
        pairs += [(i % size, (i + 1) % size), ((i + 1) % size, i % size)]
    return lax.ppermute(value, "seq", pairs)


def per_device(queries, keys, values, doc_ids):
    kv = gather(across_heads(pack_kv(tag_rows(doc_ids), keys, values)))
    kv, queries = lax.optimization_barrier((kv, queries))
    even, odd = swapped(kv, 0), swapped(kv, 1)
    qs = across_heads(pack_q(queries))
    q_ids, *state = own_block(kv, qs)
    *state, ready = near_block(False, even, qs, q_ids, state)
    out = near_block(True, odd, qs, q_ids, state, ready)
    return unpack(across_heads(out))


def solution(mesh):
    return jax.shard_map(
        per_device,
        mesh=mesh,
        in_specs=(
            P(("seq", "head"), None),
            P(("seq", "head"), None),
            P(("seq", "head"), None),
            P(("seq", "head")),
        ),
        out_specs=P(("seq", "head"), None),
        check_vma=False,
    )
```
